32 devices in a mesh: section: 4 (over y, x), dp: 4 (over z), mp: 2 (over core).
Axes of the slice: x: 2, y: 2, z: 4, core: 2. Of those that a mesh axis runs over, the one named last changes fastest.
Arguments:
- activations: bfloat16 [4, 3, 768, 2048], P('section', None, 'dp'), may hold values from -6 to 6
- out_grad: bfloat16 [3, 768, 2048], P(None, 'dp'), may hold values from -6 to 6
- weight_in: bfloat16 [4, 2048, 4096], P('section', 'dp', 'mp'), may hold values from -0.125 to 0.125
- weight_out: bfloat16 [4, 4096, 2048], P('section', 'mp', 'dp'), may hold values from -0.09375 to 0.09375
- lengths: int32 [3, 4], P(None, 'dp'), may hold values from 48 to 192, as said below
Outputs:
- input_grads: bfloat16 [4, 3, 768, 2048], P('section', None, 'dp', 'mp')
- grad_weight_in: bfloat16 [4, 2048, 4096], P('section', 'dp', 'mp')
- grad_weight_out: bfloat16 [4, 4096, 2048], P('section', 'mp', 'dp')
The draws below stay inside these ranges and needn't reach their ends.
Inputs may be any that keep to these rules, and one draw needn't show every extreme that they name: `lengths`: some replica holds a full micro-batch of 192 live tokens in every draw.
All inputs are finite; a program needn't handle non-finite values.
Results may differ from the reference program's by a relative error of at most 0.0095.
Values may be sent and summed in bfloat16 or wider, within the bound.
A program may use at most 192 MiB of HBM per device.

```python
import jax
import jax.numpy as jnp

D = 2048
FFW = 4096
MB = 3
ROWS = 192
TOKENS = 768
N_SECTION = 4
N_DP = 4


def draw_lengths(key, part):
    base = jax.random.randint(key, (MB, N_DP), ROWS // 4, ROWS + 1)
    picked = jax.random.randint(jax.random.fold_in(key, 7), (), 0, MB)
    column = jax.random.randint(jax.random.fold_in(key, 11), (), 0, N_DP)
    return base.at[picked, column].set(ROWS).astype(jnp.int32)


def shard_levels(key, shape, split, least, largest):
    level = 1.0
    for position, parts in split:
        heights = jax.random.uniform(jax.random.fold_in(jax.random.fold_in(key, 6), position), (parts,), jnp.float32, least / len(split), largest / len(split))
        level = level * jnp.repeat(jnp.exp(heights), shape[position] // parts).reshape((-1,) + (1,) * (len(shape) - 1 - position))
    return level


def bell_draw(own_key, extent, width, limit, shards=(), held_as=jnp.bfloat16):
    values = jax.random.normal(own_key, extent, jnp.float32) * width
    if len(shards) > 0:
        values = shard_levels(own_key, extent, shards, -0.22, 0.18) * values
    return jnp.clip(values, min=-limit, max=limit).astype(held_as)


def setup_inputs(seed: int = 0) -> dict:
    arg_keys = jax.random.split(jax.random.key(seed), 6)
    activations = bell_draw(arg_keys[0], (N_SECTION, MB, TOKENS, D), 1.0, 6.0, ((0, 4), (2, 4)))
    out_grad = bell_draw(arg_keys[1], (MB, TOKENS, D), 1.0, 6.0, ((1, 4),))
    weight_in = bell_draw(arg_keys[2], (N_SECTION, D, FFW), D ** -0.5, 0.125, ((0, 4), (1, 4), (2, 2)))
    weight_out = bell_draw(arg_keys[3], (N_SECTION, FFW, D), FFW ** -0.5, 0.09375, ((0, 4), (1, 2), (2, 4)))
    lengths = draw_lengths(jax.random.fold_in(arg_keys[5], 71), 0)
    return dict(activations=activations, out_grad=out_grad, weight_in=weight_in, weight_out=weight_out, lengths=lengths)


def reference(activations, out_grad, weight_in, weight_out, lengths):
    limits = jnp.repeat(lengths, ROWS, axis=1)
    valid = (jnp.arange(TOKENS)[None, :] % ROWS) < limits
    grad = jnp.where(valid[..., None], out_grad, jnp.zeros_like(out_grad)).reshape(-1, D)
    grads_list = []
    dw_in_list = []
    dw_out_list = []
    for section_index in range(N_SECTION - 1, -1, -1):
        inputs = activations[section_index].reshape(-1, D)
        pre = jnp.dot(inputs, weight_in[section_index], preferred_element_type=jnp.float32)
        sigma = jax.nn.sigmoid(pre)
        act = (pre * sigma).astype(jnp.bfloat16)
        grad_act = jnp.dot(grad, weight_out[section_index].T, preferred_element_type=jnp.float32)
        dpre = (grad_act * sigma * (1.0 + pre * (1.0 - sigma))).astype(jnp.bfloat16)
        back = jnp.dot(dpre, weight_in[section_index].T, preferred_element_type=jnp.float32)
        dw_in_list.append(jnp.dot(inputs.T, dpre, preferred_element_type=jnp.float32).astype(jnp.bfloat16))
        dw_out_list.append(jnp.dot(act.T, grad, preferred_element_type=jnp.float32).astype(jnp.bfloat16))
        grad = (grad.astype(jnp.float32) + back).astype(jnp.bfloat16)
        grads_list.append(grad.reshape(MB, TOKENS, D))
    input_grads = jnp.stack(grads_list[::-1])
    grad_weight_in = jnp.stack(dw_in_list[::-1])
    grad_weight_out = jnp.stack(dw_out_list[::-1])
    return input_grads, grad_weight_in, grad_weight_out
```

```python
import jax
import jax.numpy as jnp
from jax import lax
from jax.sharding import PartitionSpec as P


def passed_along(x, axis, by):
    devices = lax.axis_size(axis)
    pairs = [(i, i + by) for i in range(devices) if 0 <= i + by < devices]
    return lax.ppermute(x, axis, pairs)


def swapped(x):
    return lax.ppermute(x, "mp", [(0, 1), (1, 0)])


def cross(left, right):
    return lax.dot_general(
        left, right, (((0,), (0,)), ((), ())), preferred_element_type=jnp.float32
    )


def times_transposed(left, right):
    return lax.dot_general(
        left, right, (((1,), (1,)), ((), ())), preferred_element_type=jnp.float32
    )


def both_halves(x):
    other = swapped(x)
    first = lax.axis_index("mp") == 0
    return jnp.concatenate([jnp.where(first, x, other), jnp.where(first, other, x)], axis=-1)


def slope(pre):
    sigma = jax.nn.sigmoid(pre)
    return sigma * (1.0 + pre * (1.0 - sigma))


def local(activations, out_grad, weight_in, weight_out, lengths):
    sections = lax.axis_size("section")
    section_index = lax.axis_index("section")
    mp_count = lax.axis_size("mp")
    mp_index = lax.axis_index("mp")
    dp_count = lax.axis_size("dp")
    dp_index = lax.axis_index("dp")
    micro_count, row_count, width = out_grad.shape
    half = width // mp_count
    part = weight_in.shape[1]
    hidden = weight_in.shape[2]
    saved = activations[0]
    full_in = lax.all_gather(weight_in[0], "dp", axis=0, tiled=True)
    full_out = lax.all_gather(weight_out[0], "dp", axis=1, tiled=True)
    valid = jnp.arange(row_count)[None, :] < lengths
    own_grad = lax.dynamic_slice_in_dim(out_grad, mp_index * half, half, 2)
    own_grad = jnp.where(valid[..., None], own_grad, jnp.zeros_like(own_grad))
    own_saved = lax.dynamic_slice_in_dim(saved, mp_index * half, half, 2)
    pre = jnp.dot(saved.reshape(-1, width), full_in, preferred_element_type=jnp.float32)
    slopes = slope(pre).reshape(micro_count, row_count, hidden)

    incoming = jnp.zeros((row_count, half), jnp.bfloat16)
    grads = jnp.zeros((micro_count, row_count, half), jnp.bfloat16)
    arrived = jnp.zeros((micro_count, row_count, half), jnp.bfloat16)
    for clock in range(sections + micro_count - 1):
        micro = clock - (sections - 1 - section_index)
        active = (micro >= 0) & (micro < micro_count)
        slot = jnp.clip(micro, 0, micro_count - 1)
        first = lax.dynamic_index_in_dim(own_grad, slot, 0, keepdims=False)
        own = jnp.where(section_index == sections - 1, first, incoming)
        grad_act = times_transposed(both_halves(own), full_out)
        scale = lax.dynamic_index_in_dim(slopes, slot, 0, keepdims=False)
        dpre = (grad_act * scale).astype(jnp.bfloat16)
        terms = times_transposed(dpre, full_in)
        mine = lax.dynamic_slice_in_dim(terms, mp_index * half, half, 1)
        theirs = lax.dynamic_slice_in_dim(terms, (1 - mp_index) * half, half, 1)
        result = own.astype(jnp.float32) + (
            mine + swapped(theirs.astype(jnp.bfloat16)).astype(jnp.float32)
        )
        result = result.astype(jnp.bfloat16)
        if clock < sections + micro_count - 2:
            incoming = passed_along(result, "section", -1)
        grads = jnp.where(active, lax.dynamic_update_index_in_dim(grads, result, slot, 0), grads)
        arrived = jnp.where(active, lax.dynamic_update_index_in_dim(arrived, own, slot, 0), arrived)

    all_saved = lax.all_gather(own_saved, "dp", axis=0, tiled=True)
    all_saved = all_saved.reshape(-1, row_count, half)
    all_grad = lax.all_gather(arrived, "dp", axis=0, tiled=True)
    all_grad = all_grad.reshape(-1, row_count, half)

    chunk = min(4, dp_count)
    steps = micro_count * dp_count // chunk
    rows = chunk * row_count
    total_in = jnp.zeros((part, hidden), jnp.float32)
    total_out = jnp.zeros((hidden, part), jnp.float32)

    def tail(x, g, total_in, total_out):
        x, g = both_halves(x.reshape(rows, half)), both_halves(g.reshape(rows, half))
        pre = jnp.dot(x, full_in, preferred_element_type=jnp.float32)
        sigma = jax.nn.sigmoid(pre)
        act = (pre * sigma).astype(jnp.bfloat16)
        grad_act = times_transposed(g, full_out)
        dpre = (grad_act * sigma * (1.0 + pre * (1.0 - sigma))).astype(jnp.bfloat16)
        x_part = lax.dynamic_slice_in_dim(x, dp_index * part, part, 1)
        g_part = lax.dynamic_slice_in_dim(g, dp_index * part, part, 1)
        return total_in + cross(x_part, dpre), total_out + cross(act, g_part)

    if steps <= 4:
        for i in range(steps):
            total_in, total_out = tail(
                all_saved[i * chunk : (i + 1) * chunk],
                all_grad[i * chunk : (i + 1) * chunk],
                total_in,
                total_out,
            )
    else:
        def body(i, totals):
            x = lax.dynamic_slice_in_dim(all_saved, i * chunk, chunk, 0)
            g = lax.dynamic_slice_in_dim(all_grad, i * chunk, chunk, 0)
            return tail(x, g, *totals)

        total_in, total_out = lax.fori_loop(0, steps, body, (total_in, total_out))
    return (
        grads[None],
        total_in.astype(jnp.bfloat16)[None],
        total_out.astype(jnp.bfloat16)[None],
    )


def solution(mesh):
    return jax.shard_map(
        local,
        mesh=mesh,
        in_specs=(
            P("section", None, "dp", None),
            P(None, "dp", None),
            P("section", "dp", "mp"),
            P("section", "mp", "dp"),
            P(None, "dp"),
        ),
        out_specs=(
            P("section", None, "dp", "mp"),
            P("section", "dp", "mp"),
            P("section", "mp", "dp"),
        ),
        check_vma=False,
    )
```

```python
import functools

import jax
import jax.numpy as jnp
from jax import lax
from jax.experimental import pallas as pl
from jax.experimental.pallas import tpu as pltpu
from jax.sharding import PartitionSpec as P


def passed_along(x, axis, by):
    devices = lax.axis_size(axis)
    pairs = [(i, i + by) for i in range(devices) if 0 <= i + by < devices]
    return lax.ppermute(x, axis, pairs)


def swapped(x):
    return lax.ppermute(x, "mp", [(0, 1), (1, 0)])


def cross(left, right):
    return lax.dot_general(
        left, right, (((0,), (0,)), ((), ())), preferred_element_type=jnp.float32
    )


def times_transposed(left, right):
    return lax.dot_general(
        left, right, (((1,), (1,)), ((), ())), preferred_element_type=jnp.float32
    )


def both_halves(x):
    other = swapped(x)
    first = lax.axis_index("mp") == 0
    return jnp.concatenate([jnp.where(first, x, other), jnp.where(first, other, x)], axis=-1)


def slope(pre):
    sigma = jax.nn.sigmoid(pre)
    return sigma * (1.0 + pre * (1.0 - sigma))


MESH = pl.DeviceIdType.MESH
TILE = 512


def chain_kernel(
    sections, replicas, w_in, w_out, slopes, first, own_x,
    grads, all_x, all_g,
    g_buf, dpre, mine, give, take,
    hop_send, hop_recv, fwd_send, fwd_recv, swap_send, swap_recv,
    x_send, x_recv, g_send, g_recv, own_sem,
):
    section = lax.axis_index("section")
    place = lax.axis_index("dp")
    core = lax.axis_index("mp")
    micros, _, rows, half = g_buf.shape
    hidden = dpre.shape[1]
    last = sections - 1

    barrier = pltpu.get_barrier_semaphore()
    greeted = [{"mp": 1 - core}]
    greeted += [{"dp": lax.rem(place + step, replicas)} for step in (1, replicas - 1)]
    greeted += [{"section": lax.rem(section + step, sections)} for step in (1, sections - 1)]
    for device in greeted:
        pl.semaphore_signal(barrier, inc=1, device_id=device, device_id_type=MESH)
    pl.semaphore_wait(barrier, len(greeted))

    def remote(src, dst, send, recv, device):
        return pltpu.make_async_remote_copy(
            src_ref=src, dst_ref=dst, send_sem=send, recv_sem=recv,
            device_id=device, device_id_type=MESH,
        )

    def sent(way, k):
        origin = place - (k - 1) if way == 0 else place + (k - 1)
        to = place + 1 if way == 0 else place - 1
        ok = (origin >= 0) & (origin < replicas) & (to >= 0) & (to < replicas)
        return jnp.clip(origin, 0, replicas - 1), jnp.clip(to, 0, replicas - 1), ok

    def came(way, k):
        origin = place - k if way == 0 else place + k
        return jnp.clip(origin, 0, replicas - 1), (origin >= 0) & (origin < replicas)

    def x_copy(way, k, origin, to):
        src = own_x if k == 1 else all_x.at[origin]
        return remote(
            src, all_x.at[origin], x_send.at[way, k - 1], x_recv.at[way, k - 1], {"dp": to}
        )

    def g_copy(way, k, m, origin, to):
        src = g_buf.at[m, core] if k == 1 else all_g.at[origin, m]
        return remote(
            src, all_g.at[origin, m], g_send.at[way, k - 1, m], g_recv.at[way, k - 1, m],
            {"dp": to},
        )

    def start(copy_of, k, *m):
        for way in range(2):
            origin, to, ok = sent(way, k)

            @pl.when(ok)
            def _():
                copy_of(way, k, *m, origin, to).start()

    def landed(copy_of, k, *m):
        for way in range(2):
            origin, ok = came(way, k)

            @pl.when(ok)
            def _():
                copy_of(way, k, *m, origin, origin).wait_recv()

    def left(copy_of, k, *m):
        for way in range(2):
            origin, to, ok = sent(way, k)

            @pl.when(ok)
            def _():
                copy_of(way, k, *m, origin, to).wait_send()

    def hop(m):
        return remote(
            grads.at[m], g_buf.at[m, core], hop_send.at[m], hop_recv.at[m],
            {"section": jnp.maximum(section - 1, 0)},
        )

    def forward(m, which):
        return remote(
            g_buf.at[m, which], g_buf.at[m, which], fwd_send.at[m], fwd_recv.at[m],
            {"mp": 1 - core},
        )

    def swap(m):
        return remote(
            give.at[m], take.at[m], swap_send.at[m], swap_recv.at[m], {"mp": 1 - core}
        )

    def own_copies(m):
        return pltpu.make_async_copy(g_buf.at[m, core], all_g.at[place, m], own_sem.at[m])

    def nt(left_block, right_block):
        return lax.dot_general(
            left_block, right_block, (((1,), (1,)), ((), ())),
            preferred_element_type=jnp.float32,
        )

    start(x_copy, 1)
    x_own = pltpu.make_async_copy(own_x, all_x.at[place], own_sem.at[micros])
    x_own.start()
    for k in range(2, replicas):

        @pl.when(section <= last - k)
        def _():
            landed(x_copy, k - 1)
            start(x_copy, k)

    for m in range(micros):

        @pl.when(section == last)
        def _():
            g_buf[m] = first[m]

        @pl.when(section < last)
        def _():
            hop(m).wait_recv()
            forward(m, core).start()

        start(g_copy, 1, m)
        own_copies(m).start()

        @pl.when(section < last)
        def _():
            forward(m, 1 - core).wait_recv()

        @pl.loop(0, hidden // TILE)
        def _(j):
            at = pl.ds(pl.multiple_of(j * TILE, TILE), TILE)
            total = nt(g_buf[m, 0], w_out[at, :half]) + nt(g_buf[m, 1], w_out[at, half:])
            dpre[:, at] = (total * slopes[m, :, at]).astype(jnp.bfloat16)

        @pl.loop(0, half // TILE)
        def _(j):
            at = pl.ds(pl.multiple_of(j * TILE, TILE), TILE)
            there = pl.ds(pl.multiple_of((1 - core) * half + j * TILE, TILE), TILE)
            give[m, :, at] = nt(dpre[...], w_in[there, :]).astype(jnp.bfloat16)

        swap(m).start()

        @pl.loop(0, half // TILE)
        def _(j):
            at = pl.ds(pl.multiple_of(j * TILE, TILE), TILE)
            here = pl.ds(pl.multiple_of(core * half + j * TILE, TILE), TILE)
            mine[:, at] = nt(dpre[...], w_in[here, :])

        swap(m).wait_recv()
        grads[m] = (
            g_buf[m, core].astype(jnp.float32) + (mine[...] + take[m].astype(jnp.float32))
        ).astype(jnp.bfloat16)

        @pl.when(section > 0)
        def _():
            hop(m).start()

    for k in range(2, replicas):

        @pl.when(section > last - k)
        def _():
            landed(x_copy, k - 1)
            start(x_copy, k)

    for k in range(2, replicas):
        for m in range(micros):
            landed(g_copy, k - 1, m)
            start(g_copy, k, m)
    landed(x_copy, replicas - 1)
    for m in range(micros):
        landed(g_copy, replicas - 1, m)
    x_own.wait()
    for m in range(micros):
        own_copies(m).wait()
        swap(m).wait_send()

        @pl.when(section < last)
        def _():
            forward(m, core).wait_send()

        @pl.when(section > 0)
        def _():
            hop(m).wait_send()

    for k in range(1, replicas):
        left(x_copy, k)
        for m in range(micros):
            left(g_copy, k, m)


def chain(sections, replicas, full_in, full_out, slopes, first, own_x):
    micros, cores, rows, half = first.shape
    hidden = full_out.shape[0]
    vmem, hbm = pl.BlockSpec(memory_space=pltpu.VMEM), pl.BlockSpec(memory_space=pl.ANY)
    dma = pltpu.SemaphoreType.DMA
    everyone = jax.ShapeDtypeStruct((replicas, micros, rows, half), jnp.bfloat16)
    block = (micros, rows, half)
    return pl.pallas_call(
        functools.partial(chain_kernel, sections, replicas),
        out_shape=(jax.ShapeDtypeStruct(block, jnp.bfloat16), everyone, everyone),
        in_specs=[vmem, vmem, vmem, vmem, hbm],
        out_specs=(vmem, hbm, hbm),
        scratch_shapes=[
            pltpu.VMEM(first.shape, jnp.bfloat16),
            pltpu.VMEM((rows, hidden), jnp.bfloat16),
            pltpu.VMEM((rows, half), jnp.float32),
            pltpu.VMEM(block, jnp.bfloat16),
            pltpu.VMEM(block, jnp.bfloat16),
        ]
        + [dma((micros,))] * 6
        + [dma((2, replicas - 1))] * 2
        + [dma((2, replicas - 1, micros))] * 2
        + [dma((micros + 1,))],
        compiler_params=pltpu.CompilerParams(
            collective_id=0, has_side_effects=True, vmem_limit_bytes=56 * 1024 * 1024
        ),
        cost_estimate=pl.CostEstimate(
            flops=8 * micros * rows * half * hidden * cores,
            bytes_accessed=8 * full_in.size,
            transcendentals=0,
        ),
    )(full_in, full_out, slopes, first, own_x)


def local(activations, out_grad, weight_in, weight_out, lengths):
    sections = lax.axis_size("section")
    section_index = lax.axis_index("section")
    mp_count = lax.axis_size("mp")
    mp_index = lax.axis_index("mp")
    dp_count = lax.axis_size("dp")
    dp_index = lax.axis_index("dp")
    micro_count, row_count, width = out_grad.shape
    half = width // mp_count
    part = weight_in.shape[1]
    hidden = weight_in.shape[2]
    saved = activations[0]
    full_in = lax.all_gather(weight_in[0], "dp", axis=0, tiled=True)
    full_out = lax.all_gather(weight_out[0], "dp", axis=1, tiled=True)
    valid = jnp.arange(row_count)[None, :] < lengths
    own_saved = lax.dynamic_slice_in_dim(saved, mp_index * half, half, 2)
    pre = jnp.dot(saved.reshape(-1, width), full_in, preferred_element_type=jnp.float32)
    slopes = slope(pre).reshape(micro_count, row_count, hidden)

    first = out_grad.reshape(micro_count, row_count, mp_count, half)
    first = jnp.where(valid[..., None, None], first, jnp.zeros_like(first)).transpose(0, 2, 1, 3)
    grads, all_saved, all_grad = chain(
        sections, dp_count, full_in, full_out, slopes, first, own_saved
    )
    all_saved = all_saved.reshape(-1, row_count, half)
    all_grad = all_grad.reshape(-1, row_count, half)

    chunk = min(4, dp_count)
    steps = micro_count * dp_count // chunk
    rows = chunk * row_count
    total_in = jnp.zeros((part, hidden), jnp.float32)
    total_out = jnp.zeros((hidden, part), jnp.float32)

    def tail(x, g, total_in, total_out):
        x, g = both_halves(x.reshape(rows, half)), both_halves(g.reshape(rows, half))
        pre = jnp.dot(x, full_in, preferred_element_type=jnp.float32)
        sigma = jax.nn.sigmoid(pre)
        act = (pre * sigma).astype(jnp.bfloat16)
        grad_act = times_transposed(g, full_out)
        dpre = (grad_act * sigma * (1.0 + pre * (1.0 - sigma))).astype(jnp.bfloat16)
        x_part = lax.dynamic_slice_in_dim(x, dp_index * part, part, 1)
        g_part = lax.dynamic_slice_in_dim(g, dp_index * part, part, 1)
        return total_in + cross(x_part, dpre), total_out + cross(act, g_part)

    if steps <= 4:
        for i in range(steps):
            total_in, total_out = tail(
                all_saved[i * chunk : (i + 1) * chunk],
                all_grad[i * chunk : (i + 1) * chunk],
                total_in,
                total_out,
            )
    else:
        def body(i, totals):
            x = lax.dynamic_slice_in_dim(all_saved, i * chunk, chunk, 0)
            g = lax.dynamic_slice_in_dim(all_grad, i * chunk, chunk, 0)
            return tail(x, g, *totals)

        total_in, total_out = lax.fori_loop(0, steps, body, (total_in, total_out))
    return (
        grads[None],
        total_in.astype(jnp.bfloat16)[None],
        total_out.astype(jnp.bfloat16)[None],
    )


def solution(mesh):
    return jax.shard_map(
        local,
        mesh=mesh,
        in_specs=(
            P("section", None, "dp", None),
            P(None, "dp", None),
            P("section", "dp", "mp"),
            P("section", "mp", "dp"),
            P(None, "dp"),
        ),
        out_specs=(
            P("section", None, "dp", "mp"),
            P("section", "dp", "mp"),
            P("section", "mp", "dp"),
        ),
        check_vma=False,
    )
```

```python
import functools

import jax
import jax.numpy as jnp
from jax import lax
from jax.experimental import pallas as pl
from jax.experimental.pallas import tpu as pltpu
from jax.sharding import PartitionSpec as P


def slope(pre):
    sigma = jax.nn.sigmoid(pre)
    return sigma * (1.0 + pre * (1.0 - sigma))


MESH = pl.DeviceIdType.MESH
TILE = 512
UNIT = 256


def chain_kernel(
    sections, replicas, w_in, w_out, slopes, first, own_x,
    grads, dw_in, dw_out, all_x, all_g,
    g_buf, dpre, mine, give, take, x_now, g_now, x_turned, sum_in, sum_out,
    hop_send, hop_recv, fwd_send, fwd_recv, swap_send, swap_recv,
    x_send, x_recv, x_give, x_take, g_send, g_recv, g_give, g_take, load_sem,
):
    section = lax.axis_index("section")
    place = lax.axis_index("dp")
    core = lax.axis_index("mp")
    micros, _, rows, half = g_buf.shape
    hidden = dpre.shape[1]
    part = dw_in.shape[0]
    last = sections - 1

    barrier = pltpu.get_barrier_semaphore()
    greeted = [{"mp": 1 - core}]
    greeted += [{"dp": lax.rem(place + step, replicas)} for step in (1, replicas - 1)]
    greeted += [{"section": lax.rem(section + step, sections)} for step in (1, sections - 1)]
    for device in greeted:
        pl.semaphore_signal(barrier, inc=1, device_id=device, device_id_type=MESH)
    pl.semaphore_wait(barrier, len(greeted))

    def remote(src, dst, send, recv, device):
        return pltpu.make_async_remote_copy(
            src_ref=src, dst_ref=dst, send_sem=send, recv_sem=recv,
            device_id=device, device_id_type=MESH,
        )

    def sent(way, k):
        sign = 1 - 2 * way
        origin, to = place - sign * (k - 1), place + sign
        ok = (origin >= 0) & (origin < replicas) & (to >= 0) & (to < replicas)
        return jnp.clip(origin, 0, replicas - 1), jnp.clip(to, 0, replicas - 1), ok

    def came(way, k):
        origin = place - (1 - 2 * way) * k
        return jnp.clip(origin, 0, replicas - 1), (origin >= 0) & (origin < replicas)

    def own_stage(k):
        return isinstance(k, int) and k == 1

    def x_copy(way, k, origin, to):
        there = all_x.at[origin, core]
        src = own_x.at[core] if own_stage(k) else there
        return remote(src, there, x_send.at[way, k - 1], x_recv.at[way, k - 1], {"dp": to})

    def g_copy(way, k, m, origin, to):
        there = all_g.at[origin, core, pl.ds(m * rows, rows)]
        src = g_buf.at[m, core] if own_stage(k) else there
        return remote(
            src, there, g_send.at[way, k - 1, m], g_recv.at[way, k - 1, m], {"dp": to}
        )

    def x_share(way, k, origin, which):
        block = all_x.at[origin, which]
        return remote(
            block, block, x_give.at[way, k - 1], x_take.at[way, k - 1], {"mp": 1 - core}
        )

    def g_share(way, k, m, origin, which):
        block = all_g.at[origin, which, pl.ds(m * rows, rows)]
        return remote(
            block, block, g_give.at[way, k - 1, m], g_take.at[way, k - 1, m], {"mp": 1 - core}
        )

    def start(copy_of, k, *m):
        for way in range(2):
            origin, to, ok = sent(way, k)

            @pl.when(ok)
            def _():
                copy_of(way, k, *m, origin, to).start()

    def landed(copy_of, share_of, k, *m):
        for way in range(2):
            origin, ok = came(way, k)

            @pl.when(ok)
            def _():
                copy_of(way, k, *m, origin, origin).wait_recv()
                share_of(way, k, *m, origin, core).start()

    def left(copy_of, share_of, k, *m):
        for way in range(2):
            origin, to, ok = sent(way, k)

            @pl.when(ok)
            def _():
                copy_of(way, k, *m, origin, to).wait_send()

            source, here = came(way, k)

            @pl.when(here)
            def _():
                share_of(way, k, *m, source, core).wait_send()

    def hop(m):
        return remote(
            grads.at[m], g_buf.at[m, core], hop_send.at[m], hop_recv.at[m],
            {"section": jnp.maximum(section - 1, 0)},
        )

    def forward(m, which):
        return remote(
            g_buf.at[m, which], g_buf.at[m, which], fwd_send.at[m], fwd_recv.at[m],
            {"mp": 1 - core},
        )

    def swap(m):
        return remote(
            give.at[m], take.at[m], swap_send.at[m], swap_recv.at[m], {"mp": 1 - core}
        )

    def nt(left_block, right_block):
        return lax.dot_general(
            left_block, right_block, (((1,), (1,)), ((), ())),
            preferred_element_type=jnp.float32,
        )

    def nn(left_block, right_block):
        return jnp.dot(left_block, right_block, preferred_element_type=jnp.float32)

    start(x_copy, 1)
    sum_in[...] = jnp.zeros_like(sum_in)
    sum_out[...] = jnp.zeros_like(sum_out)
    for k in range(2, replicas):

        @pl.when(section <= last - k)
        def _():
            landed(x_copy, x_share, k - 1)
            start(x_copy, k)

    for m in range(micros):

        @pl.when(section == last)
        def _():
            g_buf[m] = first[m]

        @pl.when(section < last)
        def _():
            hop(m).wait_recv()
            forward(m, core).start()

        start(g_copy, 1, m)

        @pl.when(section < last)
        def _():
            forward(m, 1 - core).wait_recv()

        @pl.loop(0, hidden // TILE)
        def _(j):
            at = pl.ds(pl.multiple_of(j * TILE, TILE), TILE)
            total = nt(g_buf[m, 0], w_out[at, :half]) + nt(g_buf[m, 1], w_out[at, half:])
            dpre[:, at] = (total * slopes[m, :, at]).astype(jnp.bfloat16)

        @pl.loop(0, half // TILE)
        def _(j):
            at = pl.ds(pl.multiple_of(j * TILE, TILE), TILE)
            there = pl.ds(pl.multiple_of((1 - core) * half + j * TILE, TILE), TILE)
            give[m, :, at] = nt(dpre[...], w_in[there, :]).astype(jnp.bfloat16)

        swap(m).start()

        @pl.loop(0, half // TILE)
        def _(j):
            at = pl.ds(pl.multiple_of(j * TILE, TILE), TILE)
            here = pl.ds(pl.multiple_of(core * half + j * TILE, TILE), TILE)
            mine[:, at] = nt(dpre[...], w_in[here, :])

        swap(m).wait_recv()
        grads[m] = (
            g_buf[m, core].astype(jnp.float32) + (mine[...] + take[m].astype(jnp.float32))
        ).astype(jnp.bfloat16)

        @pl.when(section > 0)
        def _():
            hop(m).start()

    for k in range(2, replicas):

        @pl.when(section > last - k)
        def _():
            landed(x_copy, x_share, k - 1)
            start(x_copy, k)

    def weight_terms():
        column = place * part
        side = column // half
        span = pl.ds(pl.multiple_of(lax.rem(column, half), part), part)
        x_turned[...] = x_now[side, :, span].T

        @pl.loop(0, hidden // UNIT)
        def _(j):
            at = pl.ds(pl.multiple_of(j * UNIT, UNIT), UNIT)
            pre = nn(x_now[0], w_in[:half, at]) + nn(x_now[1], w_in[half:, at])
            sigma = jax.nn.sigmoid(pre)
            act = (pre * sigma).astype(jnp.bfloat16)
            total = nt(g_now[0], w_out[at, :half]) + nt(g_now[1], w_out[at, half:])
            slope_now = sigma * (1.0 + pre * (1.0 - sigma))
            dpre_now = (total * slope_now).astype(jnp.bfloat16)
            sum_in[:, at] += nn(x_turned[...], dpre_now)
            sum_out[at, :] += nn(act.T, g_now[side, :, span])

    @pl.loop(0, replicas)
    def _(k):
        @pl.when(k + 1 < replicas)
        def _():
            for m in range(micros):
                landed(g_copy, g_share, k + 1, m)

                @pl.when(k + 2 < replicas)
                def _():
                    start(g_copy, k + 2, m)

        @pl.when(k + 2 == replicas)
        def _():
            landed(x_copy, x_share, replicas - 1)

        @pl.loop(0, 2)
        def _(way):
            origin, there = came(way, k)

            @pl.when(there & ((k > 0) | (way == 0)))
            def _():
                @pl.when(k == 0)
                def _():
                    load = pltpu.make_async_copy(own_x, x_now, load_sem.at[0])
                    load.start()
                    for m in range(micros):
                        for side in range(2):
                            g_now[side, m * rows : (m + 1) * rows] = g_buf[m, side]
                    load.wait()

                @pl.when(k > 0)
                def _():
                    x_share(way, k, origin, 1 - core).wait_recv()
                    load = pltpu.make_async_copy(all_x.at[origin], x_now, load_sem.at[0])
                    load.start()
                    for m in range(micros):
                        g_share(way, k, m, origin, 1 - core).wait_recv()
                    load_g = pltpu.make_async_copy(all_g.at[origin], g_now, load_sem.at[1])
                    load_g.start()
                    load.wait()
                    load_g.wait()

                weight_terms()

    dw_in[...] = sum_in[...].astype(jnp.bfloat16)
    dw_out[...] = sum_out[...].astype(jnp.bfloat16)
    for m in range(micros):
        swap(m).wait_send()

        @pl.when(section < last)
        def _():
            forward(m, core).wait_send()

        @pl.when(section > 0)
        def _():
            hop(m).wait_send()

    for k in range(1, replicas):
        left(x_copy, x_share, k)
        for m in range(micros):
            left(g_copy, g_share, k, m)


def chain(sections, replicas, full_in, full_out, slopes, first, own_x):
    micros, cores, rows, half = first.shape
    hidden = full_out.shape[0]
    part = cores * half // replicas
    tokens = micros * rows
    vmem, hbm = pl.BlockSpec(memory_space=pltpu.VMEM), pl.BlockSpec(memory_space=pl.ANY)
    dma = pltpu.SemaphoreType.DMA
    everyone = jax.ShapeDtypeStruct((replicas, cores, tokens, half), jnp.bfloat16)
    block = (micros, rows, half)
    return pl.pallas_call(
        functools.partial(chain_kernel, sections, replicas),
        out_shape=(
            jax.ShapeDtypeStruct(block, jnp.bfloat16),
            jax.ShapeDtypeStruct((part, hidden), jnp.bfloat16),
            jax.ShapeDtypeStruct((hidden, part), jnp.bfloat16),
            everyone,
            everyone,
        ),
        in_specs=[vmem, vmem, vmem, vmem, hbm],
        out_specs=(vmem, vmem, vmem, hbm, hbm),
        scratch_shapes=[
            pltpu.VMEM(first.shape, jnp.bfloat16),
            pltpu.VMEM((rows, hidden), jnp.bfloat16),
            pltpu.VMEM((rows, half), jnp.float32),
            pltpu.VMEM(block, jnp.bfloat16),
            pltpu.VMEM(block, jnp.bfloat16),
            pltpu.VMEM((cores, tokens, half), jnp.bfloat16),
            pltpu.VMEM((cores, tokens, half), jnp.bfloat16),
            pltpu.VMEM((part, tokens), jnp.bfloat16),
            pltpu.VMEM((part, hidden), jnp.float32),
            pltpu.VMEM((hidden, part), jnp.float32),
        ]
        + [dma((micros,))] * 6
        + [dma((2, replicas - 1))] * 4
        + [dma((2, replicas - 1, micros))] * 4
        + [dma((2,))],
        compiler_params=pltpu.CompilerParams(
            collective_id=0, has_side_effects=True, vmem_limit_bytes=60 * 1024 * 1024
        ),
        cost_estimate=pl.CostEstimate(
            flops=8 * micros * rows * half * hidden * cores,
            bytes_accessed=8 * full_in.size,
            transcendentals=0,
        ),
    )(full_in, full_out, slopes, first, own_x)


def local(activations, out_grad, weight_in, weight_out, lengths):
    sections = lax.axis_size("section")
    mp_count = lax.axis_size("mp")
    dp_count = lax.axis_size("dp")
    micro_count, row_count, width = out_grad.shape
    half = width // mp_count
    hidden = weight_in.shape[2]
    saved = activations[0]
    full_in = lax.all_gather(weight_in[0], "dp", axis=0, tiled=True)
    full_out = lax.all_gather(weight_out[0], "dp", axis=1, tiled=True)
    valid = jnp.arange(row_count)[None, :] < lengths
    own_saved = saved.reshape(-1, mp_count, half).transpose(1, 0, 2)
    pre = jnp.dot(saved.reshape(-1, width), full_in, preferred_element_type=jnp.float32)
    slopes = slope(pre).reshape(micro_count, row_count, hidden)

    first = out_grad.reshape(micro_count, row_count, mp_count, half)
    first = jnp.where(valid[..., None, None], first, jnp.zeros_like(first)).transpose(0, 2, 1, 3)
    grads, dw_in, dw_out, _, _ = chain(
        sections, dp_count, full_in, full_out, slopes, first, own_saved
    )
    return grads[None], dw_in[None], dw_out[None]


def solution(mesh):
    return jax.shard_map(
        local,
        mesh=mesh,
        in_specs=(
            P("section", None, "dp", None),
            P(None, "dp", None),
            P("section", "dp", "mp"),
            P("section", "mp", "dp"),
            P(None, "dp"),
        ),
        out_specs=(
            P("section", None, "dp", "mp"),
            P("section", "dp", "mp"),
            P("section", "mp", "dp"),
        ),
        check_vma=False,
    )
```

```python
import functools

import jax
import jax.numpy as jnp
from jax import lax
from jax.experimental import pallas as pl
from jax.experimental.pallas import tpu as pltpu
from jax.sharding import PartitionSpec as P


def slope(pre):
    sigma = jax.nn.sigmoid(pre)
    return sigma * (1.0 + pre * (1.0 - sigma))


MESH = pl.DeviceIdType.MESH
TILE = 512
UNIT = 256


def chain_kernel(
    sections, replicas, own_in, own_out, first, own_x,
    grads, dw_in, dw_out, all_x, all_g,
    w_in, w_out, slopes, g_buf, dpre, mine, give, take, x_now, g_now, x_turned, sum_in, sum_out,
    hop_send, hop_recv, fwd_send, fwd_recv, swap_send, swap_recv,
    in_send, in_recv, out_send, out_recv,
    x_send, x_recv, x_give, x_take, g_send, g_recv, g_give, g_take, load_sem,
):
    section = lax.axis_index("section")
    place = lax.axis_index("dp")
    core = lax.axis_index("mp")
    micros, _, rows, half = g_buf.shape
    hidden = dpre.shape[1]
    part = dw_in.shape[0]
    last = sections - 1

    barrier = pltpu.get_barrier_semaphore()
    greeted = [{"mp": 1 - core}]
    greeted += [{"dp": lax.rem(place + step, replicas)} for step in (1, replicas - 1)]
    greeted += [{"section": lax.rem(section + step, sections)} for step in (1, sections - 1)]
    for device in greeted:
        pl.semaphore_signal(barrier, inc=1, device_id=device, device_id_type=MESH)
    pl.semaphore_wait(barrier, len(greeted))

    def remote(src, dst, send, recv, device):
        return pltpu.make_async_remote_copy(
            src_ref=src, dst_ref=dst, send_sem=send, recv_sem=recv,
            device_id=device, device_id_type=MESH,
        )

    def sent(way, k):
        sign = 1 - 2 * way
        origin, to = place - sign * (k - 1), place + sign
        ok = (origin >= 0) & (origin < replicas) & (to >= 0) & (to < replicas)
        return jnp.clip(origin, 0, replicas - 1), jnp.clip(to, 0, replicas - 1), ok

    def came(way, k):
        origin = place - (1 - 2 * way) * k
        return jnp.clip(origin, 0, replicas - 1), (origin >= 0) & (origin < replicas)

    def own_stage(k):
        return isinstance(k, int) and k == 1

    def block_of(origin):
        return pl.ds(pl.multiple_of(origin * part, part), part)

    def in_copy(way, k, origin, to):
        there = w_in.at[block_of(origin)]
        src = own_in if own_stage(k) else there
        return remote(src, there, in_send.at[way, k - 1], in_recv.at[way, k - 1], {"dp": to})

    def out_copy(way, k, origin, to):
        there = w_out.at[:, block_of(origin)]
        src = own_out if own_stage(k) else there
        return remote(src, there, out_send.at[way, k - 1], out_recv.at[way, k - 1], {"dp": to})

    def x_copy(way, k, origin, to):
        there = all_x.at[origin, core]
        src = own_x.at[core] if own_stage(k) else there
        return remote(src, there, x_send.at[way, k - 1], x_recv.at[way, k - 1], {"dp": to})

    def g_copy(way, k, m, origin, to):
        there = all_g.at[origin, core, pl.ds(m * rows, rows)]
        src = g_buf.at[m, core] if own_stage(k) else there
        return remote(
            src, there, g_send.at[way, k - 1, m], g_recv.at[way, k - 1, m], {"dp": to}
        )

    def x_share(way, k, origin, which):
        block = all_x.at[origin, which]
        return remote(
            block, block, x_give.at[way, k - 1], x_take.at[way, k - 1], {"mp": 1 - core}
        )

    def g_share(way, k, m, origin, which):
        block = all_g.at[origin, which, pl.ds(m * rows, rows)]
        return remote(
            block, block, g_give.at[way, k - 1, m], g_take.at[way, k - 1, m], {"mp": 1 - core}
        )

    def start(copy_of, k, *m):
        for way in range(2):
            origin, to, ok = sent(way, k)

            @pl.when(ok)
            def _():
                copy_of(way, k, *m, origin, to).start()

    def landed(copy_of, share_of, k, *m):
        for way in range(2):
            origin, ok = came(way, k)

            @pl.when(ok)
            def _():
                copy_of(way, k, *m, origin, origin).wait_recv()
                if share_of is not None:
                    share_of(way, k, *m, origin, core).start()

    def left(copy_of, share_of, k, *m):
        for way in range(2):
            origin, to, ok = sent(way, k)

            @pl.when(ok)
            def _():
                copy_of(way, k, *m, origin, to).wait_send()

            source, here = came(way, k)

            if share_of is not None:

                @pl.when(here)
                def _():
                    share_of(way, k, *m, source, core).wait_send()

    def hop(m):
        return remote(
            grads.at[m], g_buf.at[m, core], hop_send.at[m], hop_recv.at[m],
            {"section": jnp.maximum(section - 1, 0)},
        )

    def forward(m, which):
        return remote(
            g_buf.at[m, which], g_buf.at[m, which], fwd_send.at[m], fwd_recv.at[m],
            {"mp": 1 - core},
        )

    def swap(m):
        return remote(
            give.at[m], take.at[m], swap_send.at[m], swap_recv.at[m], {"mp": 1 - core}
        )

    def nt(left_block, right_block):
        return lax.dot_general(
            left_block, right_block, (((1,), (1,)), ((), ())),
            preferred_element_type=jnp.float32,
        )

    def nn(left_block, right_block):
        return jnp.dot(left_block, right_block, preferred_element_type=jnp.float32)

    def pre_terms(origin, fresh):
        column = origin * part
        span = pl.ds(pl.multiple_of(lax.rem(column, half), part), part)

        @pl.loop(0, hidden // TILE)
        def _(j):
            at = pl.ds(pl.multiple_of(j * TILE, TILE), TILE)
            terms = nn(x_now[column // half, :, span], w_in[block_of(origin), at])
            slopes[:, at] = terms if fresh else slopes[:, at] + terms

    start(in_copy, 1)
    start(out_copy, 1)
    loads = [
        pltpu.make_async_copy(own_in, w_in.at[block_of(place)], load_sem.at[0]),
        pltpu.make_async_copy(own_x, x_now, load_sem.at[1]),
        pltpu.make_async_copy(own_out, w_out.at[:, block_of(place)], load_sem.at[2]),
    ]
    for load in loads:
        load.start()
    for load in loads:
        load.wait()
    pre_terms(place, True)
    sum_in[...] = jnp.zeros_like(sum_in)
    sum_out[...] = jnp.zeros_like(sum_out)
    for k in range(1, replicas):
        for copy_of in (in_copy, out_copy):
            landed(copy_of, None, k)
            if k + 1 < replicas:
                start(copy_of, k + 1)
        if k == replicas - 2:
            start(x_copy, 1)
        for way in range(2):
            origin, there = came(way, k)

            @pl.when(there)
            def _():
                pre_terms(origin, False)

    @pl.loop(0, hidden // TILE)
    def _(j):
        at = pl.ds(pl.multiple_of(j * TILE, TILE), TILE)
        slopes[:, at] = slope(slopes[:, at])

    for k in range(2, replicas):

        @pl.when(section <= last - k)
        def _():
            landed(x_copy, x_share, k - 1)
            start(x_copy, k)

    for m in range(micros):

        @pl.when(section == last)
        def _():
            g_buf[m] = first[m]

        @pl.when(section < last)
        def _():
            hop(m).wait_recv()
            forward(m, core).start()

        start(g_copy, 1, m)

        @pl.when(section < last)
        def _():
            forward(m, 1 - core).wait_recv()

        @pl.loop(0, hidden // TILE)
        def _(j):
            at = pl.ds(pl.multiple_of(j * TILE, TILE), TILE)
            total = nt(g_buf[m, 0], w_out[at, :half]) + nt(g_buf[m, 1], w_out[at, half:])
            dpre[:, at] = (total * slopes[pl.ds(m * rows, rows), at]).astype(jnp.bfloat16)

        @pl.loop(0, half // TILE)
        def _(j):
            at = pl.ds(pl.multiple_of(j * TILE, TILE), TILE)
            there = pl.ds(pl.multiple_of((1 - core) * half + j * TILE, TILE), TILE)
            give[m, :, at] = nt(dpre[...], w_in[there, :]).astype(jnp.bfloat16)

        swap(m).start()

        @pl.loop(0, half // TILE)
        def _(j):
            at = pl.ds(pl.multiple_of(j * TILE, TILE), TILE)
            here = pl.ds(pl.multiple_of(core * half + j * TILE, TILE), TILE)
            mine[:, at] = nt(dpre[...], w_in[here, :])

        swap(m).wait_recv()
        grads[m] = (
            g_buf[m, core].astype(jnp.float32) + (mine[...] + take[m].astype(jnp.float32))
        ).astype(jnp.bfloat16)

        @pl.when(section > 0)
        def _():
            hop(m).start()

    for k in range(2, replicas):

        @pl.when(section > last - k)
        def _():
            landed(x_copy, x_share, k - 1)
            start(x_copy, k)

    def weight_terms():
        column = place * part
        side = column // half
        span = pl.ds(pl.multiple_of(lax.rem(column, half), part), part)
        x_turned[...] = x_now[side, :, span].T

        @pl.loop(0, hidden // UNIT)
        def _(j):
            at = pl.ds(pl.multiple_of(j * UNIT, UNIT), UNIT)
            pre = nn(x_now[0], w_in[:half, at]) + nn(x_now[1], w_in[half:, at])
            sigma = jax.nn.sigmoid(pre)
            act = (pre * sigma).astype(jnp.bfloat16)
            total = nt(g_now[0], w_out[at, :half]) + nt(g_now[1], w_out[at, half:])
            slope_now = sigma * (1.0 + pre * (1.0 - sigma))
            dpre_now = (total * slope_now).astype(jnp.bfloat16)
            sum_in[:, at] += nn(x_turned[...], dpre_now)
            sum_out[at, :] += nn(act.T, g_now[side, :, span])

    @pl.loop(0, replicas)
    def _(k):
        @pl.when(k + 1 < replicas)
        def _():
            for m in range(micros):
                landed(g_copy, g_share, k + 1, m)

                @pl.when(k + 2 < replicas)
                def _():
                    start(g_copy, k + 2, m)

        @pl.when(k + 2 == replicas)
        def _():
            landed(x_copy, x_share, replicas - 1)

        @pl.loop(0, 2)
        def _(way):
            origin, there = came(way, k)

            @pl.when(there & ((k > 0) | (way == 0)))
            def _():
                @pl.when(k == 0)
                def _():
                    for m in range(micros):
                        for side in range(2):
                            g_now[side, m * rows : (m + 1) * rows] = g_buf[m, side]

                @pl.when(k > 0)
                def _():
                    x_share(way, k, origin, 1 - core).wait_recv()
                    load = pltpu.make_async_copy(all_x.at[origin], x_now, load_sem.at[0])
                    load.start()
                    for m in range(micros):
                        g_share(way, k, m, origin, 1 - core).wait_recv()
                    load_g = pltpu.make_async_copy(all_g.at[origin], g_now, load_sem.at[1])
                    load_g.start()
                    load.wait()
                    load_g.wait()

                weight_terms()

    dw_in[...] = sum_in[...].astype(jnp.bfloat16)
    dw_out[...] = sum_out[...].astype(jnp.bfloat16)
    for m in range(micros):
        swap(m).wait_send()

        @pl.when(section < last)
        def _():
            forward(m, core).wait_send()

        @pl.when(section > 0)
        def _():
            hop(m).wait_send()

    for k in range(1, replicas):
        left(in_copy, None, k)
        left(out_copy, None, k)
        left(x_copy, x_share, k)
        for m in range(micros):
            left(g_copy, g_share, k, m)


def chain(sections, replicas, own_in, own_out, first, own_x):
    micros, cores, rows, half = first.shape
    part, hidden = own_in.shape
    width = cores * half
    tokens = micros * rows
    vmem, hbm = pl.BlockSpec(memory_space=pltpu.VMEM), pl.BlockSpec(memory_space=pl.ANY)
    dma = pltpu.SemaphoreType.DMA
    everyone = jax.ShapeDtypeStruct((replicas, cores, tokens, half), jnp.bfloat16)
    block = (micros, rows, half)
    return pl.pallas_call(
        functools.partial(chain_kernel, sections, replicas),
        out_shape=(
            jax.ShapeDtypeStruct(block, jnp.bfloat16),
            jax.ShapeDtypeStruct((part, hidden), jnp.bfloat16),
            jax.ShapeDtypeStruct((hidden, part), jnp.bfloat16),
            everyone,
            everyone,
        ),
        in_specs=[hbm, hbm, vmem, hbm],
        out_specs=(vmem, vmem, vmem, hbm, hbm),
        scratch_shapes=[
            pltpu.VMEM((width, hidden), jnp.bfloat16),
            pltpu.VMEM((hidden, width), jnp.bfloat16),
            pltpu.VMEM((tokens, hidden), jnp.float32),
            pltpu.VMEM(first.shape, jnp.bfloat16),
            pltpu.VMEM((rows, hidden), jnp.bfloat16),
            pltpu.VMEM((rows, half), jnp.float32),
            pltpu.VMEM(block, jnp.bfloat16),
            pltpu.VMEM(block, jnp.bfloat16),
            pltpu.VMEM((cores, tokens, half), jnp.bfloat16),
            pltpu.VMEM((cores, tokens, half), jnp.bfloat16),
            pltpu.VMEM((part, tokens), jnp.bfloat16),
            pltpu.VMEM((part, hidden), jnp.float32),
            pltpu.VMEM((hidden, part), jnp.float32),
        ]
        + [dma((micros,))] * 6
        + [dma((2, replicas - 1))] * 8
        + [dma((2, replicas - 1, micros))] * 4
        + [dma((3,))],
        compiler_params=pltpu.CompilerParams(
            collective_id=0, has_side_effects=True, vmem_limit_bytes=60 * 1024 * 1024
        ),
        cost_estimate=pl.CostEstimate(
            flops=8 * micros * rows * half * hidden * cores,
            bytes_accessed=8 * width * hidden,
            transcendentals=0,
        ),
    )(own_in, own_out, first, own_x)


def local(activations, out_grad, weight_in, weight_out, lengths):
    sections = lax.axis_size("section")
    mp_count = lax.axis_size("mp")
    dp_count = lax.axis_size("dp")
    micro_count, row_count, width = out_grad.shape
    half = width // mp_count
    saved = activations[0]
    valid = jnp.arange(row_count)[None, :] < lengths
    own_saved = saved.reshape(-1, mp_count, half).transpose(1, 0, 2)
    first = out_grad.reshape(micro_count, row_count, mp_count, half)
    first = jnp.where(valid[..., None, None], first, jnp.zeros_like(first)).transpose(0, 2, 1, 3)
    grads, dw_in, dw_out, _, _ = chain(
        sections, dp_count, weight_in[0], weight_out[0], first, own_saved
    )
    return grads[None], dw_in[None], dw_out[None]


def solution(mesh):
    return jax.shard_map(
        local,
        mesh=mesh,
        in_specs=(
            P("section", None, "dp", None),
            P(None, "dp", None),
            P("section", "dp", "mp"),
            P("section", "mp", "dp"),
            P(None, "dp"),
        ),
        out_specs=(
            P("section", None, "dp", "mp"),
            P("section", "dp", "mp"),
            P("section", "mp", "dp"),
        ),
        check_vma=False,
    )
```
